256 devices in a mesh: feat: 32 (over y, z), tok: 8 (over x, core).
Axes of the slice: x: 4, y: 4, z: 8, core: 2. Of those that a mesh axis runs over, the one named last changes fastest.
Arguments:
- layer_input: bfloat16 [128, 8192], P(None, 'tok'), may hold values from -6 to 6
- enc_weight: bfloat16 [8192, 32768], P('tok', 'feat'), may hold values from -0.0625 to 0.0625
- enc_bias: float32 [32768], P('feat'), may hold values from -3 to 3
- active: int32 [512, 32768], P('tok', 'feat'), may hold values 0 or 1
- dec_weight: bfloat16 [32768, 8192], P('feat', 'tok'), may hold values from -0.03125 to 0.03125
- dec_bias: float32 [8192], P('tok'), may hold values from -3 to 3
- sae_error: bfloat16 [128, 8192], P(None, 'tok'), may hold values from -3 to 3
- positions: int32 [8, 16], P('tok'), may hold values from 0 to 123, as said below
- attn_gain: float32 [8192], P('tok'), may hold values from 0.1 to 1.9
- query_weight: bfloat16 [8192, 8192], P('tok', 'feat')
- kv_weight: bfloat16 [8192, 2048], P('tok', 'feat')
- out_weight: bfloat16 [8192, 8192], P('feat', 'tok'), may hold values from -0.0625 to 0.0625
- mlp_gain: float32 [8192], P('tok'), may hold values from 0.1 to 1.9
- gate_weight: bfloat16 [8192, 16384], P('tok', 'feat'), may hold values from -0.0625 to 0.0625
- up_weight: bfloat16 [8192, 16384], P('tok', 'feat'), may hold values from -0.0625 to 0.0625
- down_weight: bfloat16 [16384, 8192], P('feat', 'tok'), may hold values from -0.046875 to 0.046875
- cotangent: bfloat16 [128, 8192], P(None, 'tok'), may hold values from -6 to 6
Outputs:
- attribution: float32 [128, 32768], P('tok', 'feat')
The draws below stay inside these ranges and needn't reach their ends.
Inputs may be any that keep to these rules, and one draw needn't show every extreme that they name: `positions`: positions rise strictly along each prompt.
All inputs are finite; a program needn't handle non-finite values. No bound on the sum of `active` on one device may be relied on, other than what follows from the above.
Results may differ from the reference program's by a relative error of at most 0.022.
Values may be sent and summed in bfloat16 or wider, within the bound.
No kernel may reach another device: no remote copies, remote signals or barrier semaphores. Data moves between devices by JAX's collectives and lax.ppermute only.
A program may use at most 64 MiB of HBM per device.

```python
import jax
import jax.numpy as jnp
from jax import lax

D = 8192
F = 32768
HF = 16384
HEADS = 64
KV = 8
HD = 128
POINTS = 4
SEQ = 16
PROMPTS = 8
ROWS = 512


def draw_positions(key, part):
    key = jax.random.fold_in(key, 5)
    first_key, gap_key = jax.random.split(key)
    first_position = jax.random.randint(first_key, (PROMPTS, 1), 0, 4)
    step_sizes = jax.random.randint(gap_key, (PROMPTS, SEQ - 1), 1, 9)
    first_position = first_position.at[0, 0].set(3)
    step_sizes = step_sizes.at[0].set(8)
    return jnp.concatenate([first_position, first_position + jnp.cumsum(step_sizes, axis=1)], axis=1).astype(jnp.int32)


def draw_query_weight(key, part):
    key = jax.random.fold_in(key, 21)
    noise_key = jax.random.fold_in(key, 0)
    noise_part = jax.random.normal(noise_key, (D, HEADS * HD), jnp.float32) * D ** (-0.5)
    return noise_part.astype(jnp.bfloat16)


def draw_kv_weight(key, part):
    key = jax.random.fold_in(key, 22)
    noise_part = jax.random.normal(key, (D, 2 * KV * HD), jnp.float32) * D ** (-0.5)
    return noise_part.astype(jnp.bfloat16)


def set_ends(entries, key, smallest, high):
    place = [jax.random.randint(jax.random.fold_in(key, axis), (), 0, length) for axis, length in enumerate(entries.shape)]
    main_axis = entries.shape.index(max(entries.shape))
    neighbour = place[:main_axis] + [(place[main_axis] + 1) % entries.shape[main_axis]] + place[main_axis + 1:]
    return entries.at[tuple(place)].set(smallest).at[tuple(neighbour)].set(high)


def steps_of(key, shape, cuts, smallest, top_value):
    def one(dim, shards_of):
        draws = jax.random.uniform(jax.random.fold_in(jax.random.fold_in(key, 6), dim), (shards_of,), jnp.float32, smallest / len(cuts), top_value / len(cuts))
        return jnp.repeat(jnp.exp(draws), shape[dim] // shards_of).reshape((-1,) + (1,) * (len(shape) - dim - 1))

    loudness = one(*cuts[0])
    for cut in cuts[1:]:
        loudness = loudness * one(*cut)
    return loudness


def gaussian(key, extent, deviation, reach, cuts=(), held_as=jnp.bfloat16):
    entries = jax.random.normal(key, extent, jnp.float32) * deviation
    if len(cuts) > 0:
        entries = steps_of(key, extent, cuts, -0.22, 0.18) * entries
    return jnp.clip(entries, min=-reach, max=reach).astype(held_as)


def setup_inputs(seed: int = 0) -> dict:
    seeds = jax.random.split(jax.random.key(seed), 18)
    return {
        "layer_input": gaussian(seeds[0], (PROMPTS * SEQ, D), 1.0, 6.0, ((1, 8),)),
        "enc_weight": gaussian(seeds[1], (D, F), D ** -0.5, 0.0625, ((0, 8), (1, 32))),
        "enc_bias": gaussian(seeds[2], (F,), 0.5, 3.0, ((0, 32),), jnp.float32),
        "active": set_ends((jax.random.randint(seeds[3], (ROWS, F), 0, 2) < 1).astype(jnp.int32), jax.random.fold_in(seeds[3], 1), 0, 1),
        "dec_weight": gaussian(seeds[4], (F, D), F ** -0.5, 0.03125, ((0, 32), (1, 8))),
        "dec_bias": gaussian(seeds[5], (D,), 0.5, 3.0, ((0, 8),), jnp.float32),
        "sae_error": gaussian(seeds[6], (PROMPTS * SEQ, D), 0.5, 3.0, ((1, 8),)),
        "positions": draw_positions(jax.random.fold_in(seeds[17], 71), 0),
        "attn_gain": jnp.clip(1.0 + 0.18 * jax.random.normal(seeds[8], (D,), jnp.float32), 0.1, 1.9),
        "query_weight": draw_query_weight(jax.random.fold_in(seeds[17], 71), 0),
        "kv_weight": draw_kv_weight(jax.random.fold_in(seeds[17], 71), 0),
        "out_weight": gaussian(seeds[11], (HEADS * HD, D), (HEADS * HD) ** -0.5, 0.0625, ((0, 32), (1, 8))),
        "mlp_gain": jnp.clip(1.0 + 0.18 * jax.random.normal(seeds[12], (D,), jnp.float32), 0.1, 1.9),
        "gate_weight": gaussian(seeds[13], (D, HF), D ** -0.5, 0.0625, ((0, 8), (1, 32))),
        "up_weight": gaussian(seeds[14], (D, HF), D ** -0.5, 0.0625, ((0, 8), (1, 32))),
        "down_weight": gaussian(seeds[15], (HF, D), HF ** -0.5, 0.046875, ((0, 32), (1, 8))),
        "cotangent": gaussian(seeds[16], (PROMPTS * SEQ, D), 1.0, 6.0, ((1, 8),)),
    }


epsilon = 1e-05
rope_base = 500000.0

def rounded(values):
    return lax.optimization_barrier(values.astype(jnp.bfloat16)).astype(jnp.float32)

def summed_products(pairs):
    running = None
    for left_side, right_side in pairs:
        product = jnp.dot(left_side, right_side, preferred_element_type=jnp.float32)
        running = product if running is None else running + product
    return running

def expand_points(values):
    last_width = values.shape[1]
    spread_out = jnp.broadcast_to(values.reshape(-1, 1, SEQ, last_width), (values.shape[0] // SEQ, POINTS, SEQ, last_width))
    return spread_out.reshape(-1, last_width)

def rotate_half(vectors, cosine_table, sine_table):
    half_width = vectors.shape[-1] // 2
    first_half = vectors[..., :half_width]
    second_half = vectors[..., half_width:]
    return jnp.concatenate([first_half * cosine_table - second_half * sine_table, second_half * cosine_table + first_half * sine_table], axis=-1)

def attend(query_rows, keyval_rows, position_rows, head_start):
    seq_count = query_rows.shape[0] // SEQ
    head_count = query_rows.shape[1] // HD
    queries = query_rows.reshape(seq_count, SEQ, head_count, HD)
    keys_all = keyval_rows[:, :KV * HD].reshape(seq_count, SEQ, KV, HD)
    values_all = keyval_rows[:, KV * HD:].reshape(seq_count, SEQ, KV, HD)
    owners = (head_start + jnp.arange(head_count, dtype=jnp.int32)) // (HEADS // KV)
    selector = (owners[:, None] == jnp.arange(KV, dtype=jnp.int32)[None, :]).astype(jnp.float32)
    key_heads = jnp.einsum('nskd,hk->nshd', keys_all, selector, precision=lax.Precision.HIGHEST)
    value_heads = jnp.einsum('nskd,hk->nshd', values_all, selector, precision=lax.Precision.HIGHEST)
    frequency = rope_base ** (-jnp.arange(HD // 2, dtype=jnp.float32) * 2.0 / HD)
    angles = position_rows.astype(jnp.float32).reshape(seq_count, SEQ, 1, 1) * frequency
    cosine_table = jnp.cos(angles)
    sine_table = jnp.sin(angles)
    queries = rotate_half(queries, cosine_table, sine_table)
    key_heads = rotate_half(key_heads, cosine_table, sine_table)
    scores = jnp.einsum('nqhd,nkhd->nhqk', queries, key_heads, precision=lax.Precision.HIGHEST) * HD ** (-0.5)
    positions_grid = position_rows.reshape(seq_count, SEQ)
    visible = positions_grid[:, None, :, None] >= positions_grid[:, None, None, :]
    scores = jnp.where(visible, scores, -1e+30)
    highest = lax.optimization_barrier(jnp.max(scores, axis=-1, keepdims=True))
    weights = jnp.exp(scores - highest)
    weights = weights / lax.optimization_barrier(jnp.sum(weights, axis=-1, keepdims=True))
    mixed_values = jnp.einsum('nhqk,nkhd->nqhd', weights, value_heads, precision=lax.Precision.HIGHEST)
    return mixed_values.reshape(seq_count * SEQ, head_count * HD)

def reference(layer_input, enc_weight, enc_bias, active, dec_weight, dec_bias, sae_error, positions, attn_gain, query_weight, kv_weight, out_weight, mlp_gain, gate_weight, up_weight, down_weight, cotangent):
    alphas = jnp.arange(1, POINTS + 1, dtype=jnp.float32) / POINTS
    encoded = summed_products([(layer_input, enc_weight)])
    pre_active = alphas[None, :, None, None] * encoded.reshape(PROMPTS, 1, SEQ, F) + enc_bias.astype(jnp.float32)
    features = active.reshape(PROMPTS, POINTS, SEQ, F).astype(jnp.float32) * pre_active
    sent_features = features.reshape(ROWS, F).astype(jnp.bfloat16)
    decoded = summed_products([(sent_features, dec_weight)])
    hidden_in = decoded + dec_bias.astype(jnp.float32) + expand_points(sae_error).astype(jnp.float32)
    scale_first = lax.rsqrt(lax.optimization_barrier(jnp.mean(hidden_in * hidden_in, axis=1, keepdims=True)) + epsilon)
    normed_first = (hidden_in * scale_first * attn_gain.astype(jnp.float32)).astype(jnp.bfloat16)
    query_rows = summed_products([(normed_first, query_weight)])
    keyval_rows = rounded(summed_products([(normed_first, kv_weight)]))
    position_rows = jnp.broadcast_to(positions.reshape(PROMPTS, 1, SEQ), (PROMPTS, POINTS, SEQ)).reshape(ROWS)
    attended, pullback = jax.vjp(lambda left_value, right_value: attend(left_value, right_value, position_rows, 0), query_rows, keyval_rows)
    projected = summed_products([(attended.astype(jnp.bfloat16), out_weight)])
    middle = hidden_in + projected
    scale_second = lax.rsqrt(lax.optimization_barrier(jnp.mean(middle * middle, axis=1, keepdims=True)) + epsilon)
    normed_second = (middle * scale_second * mlp_gain.astype(jnp.float32)).astype(jnp.bfloat16)
    gate_value = summed_products([(normed_second, gate_weight)])
    up_value = summed_products([(normed_second, up_weight)])
    back_hidden = expand_points(summed_products([(cotangent, down_weight.T)]))
    sigmoid_gate = jax.nn.sigmoid(gate_value)
    grad_gate = back_hidden * up_value * sigmoid_gate * (1.0 + gate_value * (1.0 - sigmoid_gate))
    grad_up = back_hidden * gate_value * sigmoid_gate
    back_second = summed_products([(grad_gate.astype(jnp.bfloat16), gate_weight.T), (grad_up.astype(jnp.bfloat16), up_weight.T)])
    weighted_second = back_second * mlp_gain.astype(jnp.float32)
    grad_middle = expand_points(cotangent).astype(jnp.float32) + scale_second * weighted_second - middle * scale_second ** 3 * lax.optimization_barrier(jnp.mean(weighted_second * middle, axis=1, keepdims=True))
    grad_attended = summed_products([(grad_middle.astype(jnp.bfloat16), out_weight.T)])
    grad_query, grad_keyval = pullback(grad_attended)
    back_first = summed_products([(grad_query.astype(jnp.bfloat16), query_weight.T), (grad_keyval.astype(jnp.bfloat16), kv_weight.T)])
    weighted_first = back_first * attn_gain.astype(jnp.float32)
    grad_hidden = grad_middle + scale_first * weighted_first - hidden_in * scale_first ** 3 * lax.optimization_barrier(jnp.mean(weighted_first * hidden_in, axis=1, keepdims=True))
    feature_grads = summed_products([(grad_hidden.astype(jnp.bfloat16), dec_weight.T)])
    grads_grid = feature_grads.reshape(PROMPTS, POINTS, SEQ, F)
    previous = jnp.concatenate([jnp.zeros_like(features[:, :1]), features[:, :-1]], axis=1)
    return lax.optimization_barrier(jnp.sum(grads_grid * (features - previous), axis=1)).reshape(PROMPTS * SEQ, F)
```

```python
import jax
import jax.numpy as jnp
import numpy as np
from jax import lax
from jax.sharding import Mesh
from jax.sharding import PartitionSpec as P

D = 8192
HEADS = 64
KV = 8
HD = 128
POINTS = 4
SEQ = 16
NY, NZ, NX, NC = 4, 8, 4, 2
FEAT = ("y", "z")
TOK = ("x", "c")

epsilon = 1e-05
rope_base = 500000.0
F32 = jnp.float32
B16 = jnp.bfloat16


def dot(left_side, right_side):
    return jnp.dot(left_side, right_side, preferred_element_type=F32)


def dot_t(left_side, right_side):
    return lax.dot_general(
        left_side, right_side, (((1,), (1,)), ((), ())), preferred_element_type=F32
    )


def swap(blocks, axes):
    return lax.all_to_all(blocks, axes, 0, 0, tiled=True)


def spread(piece, axes, count):
    blocks = jnp.broadcast_to(piece[None], (count,) + piece.shape)
    return swap(lax.optimization_barrier(blocks), axes).reshape((-1,) + piece.shape[1:])


def added(blocks):
    return jnp.sum(blocks.astype(F32), axis=0)


def feat_sums(partial):
    rows, width = partial.shape
    blocks = swap(partial.astype(B16).reshape(NY, rows // NY, width), "y")
    blocks = added(blocks).astype(B16).reshape(NZ, rows // (NY * NZ), width)
    return added(swap(blocks, "z"))


def feat_rows(piece):
    return spread(spread(piece, "z", NZ), "y", NY)


def tok_sums(partial):
    rows, width = partial.shape
    return added(swap(partial.astype(B16).reshape(NX * NC, rows // (NX * NC), width), TOK))


def other_core(values):
    return lax.ppermute(values, "c", [(0, 1), (1, 0)])


def tok_sums_wide(partial, core):
    rows, width = partial.shape
    blocks = partial.reshape(NX, NC, rows // (NX * NC), width)
    own = lax.dynamic_index_in_dim(blocks, core, 1, keepdims=False)
    other = lax.dynamic_index_in_dim(blocks, 1 - core, 1, keepdims=False)
    own = own + other_core(other.astype(B16)).astype(F32)
    return added(swap(own.astype(B16), "x"))


def tok_rows(piece):
    return spread(piece, TOK, NX * NC)


def tok_rows_wide(piece, core):
    own = spread(piece, "x", NX).reshape((NX,) + piece.shape)
    other = other_core(own)
    first = jnp.where(core == 0, own, other)
    second = jnp.where(core == 0, other, own)
    return jnp.stack([first, second], axis=1).reshape((-1,) + piece.shape[1:])


def split_column(values):
    high = lax.reduce_precision(values, 8, 7)
    low = values - high
    lanes = lax.broadcasted_iota(jnp.int32, (values.shape[0], 128), 1)
    return jnp.where(lanes == 0, high, jnp.where(lanes == 1, low, 0.0)).astype(B16)


def joined_column(block):
    return block[:, 0:1].astype(F32) + block[:, 1:2].astype(F32)


def row_total(values):
    partial = jnp.sum(values, axis=1, keepdims=True)
    rows = partial.shape[0]
    block = jnp.broadcast_to(partial.reshape(1, 1, rows), (NX * NC, 1, rows))
    parts = swap(lax.optimization_barrier(block), TOK)
    return jnp.sum(parts, axis=0).reshape(rows, 1)


def rotate(vectors, cosine, sine):
    half = vectors.shape[-1] // 2
    first, second = vectors[:, :half], vectors[:, half:]
    return jnp.concatenate(
        [first * cosine - second * sine, second * cosine + first * sine], axis=-1
    )


def attend(query_rows, keyval_rows, cosine, sine, visible):
    high = lax.Precision.HIGHEST
    heads = query_rows.shape[1] // HD
    keys = rotate(keyval_rows[:, :HD], cosine, sine)
    values = keyval_rows[:, HD:]
    queries = jnp.concatenate(
        [rotate(query_rows[:, h * HD : (h + 1) * HD], cosine, sine) for h in range(heads)], axis=0
    )
    scores = lax.dot_general(
        queries, keys, (((1,), (1,)), ((), ())), precision=high, preferred_element_type=F32
    ) * HD ** (-0.5)
    scores = jnp.where(visible, scores, -1e30)
    weights = jnp.exp(scores - jnp.max(scores, axis=-1, keepdims=True))
    weights = weights / jnp.sum(weights, axis=-1, keepdims=True)
    mixed = jnp.dot(weights, values, precision=high, preferred_element_type=F32)
    rows = query_rows.shape[0]
    return jnp.concatenate([mixed[h * rows : (h + 1) * rows] for h in range(heads)], axis=1)


def own_keyval_weight(kv_weight):
    feat = lax.axis_index(FEAT)
    group = lax.rem(feat, 4)
    parts = []
    for shift in range(4):
        moves = []
        for source in range(NY * NZ):
            kind = (source // 16) * 2 + source % 2
            head = (source % 16) // 2
            moves.append((source, 4 * head + (kind + shift) % 4))
        parts.append(lax.ppermute(kv_weight, FEAT, moves))
    parts = jnp.stack(parts)
    blocks = [
        lax.dynamic_index_in_dim(parts, lax.rem(group - kind + 4, 4), 0, keepdims=False)
        for kind in range(4)
    ]
    return jnp.concatenate(blocks, axis=1)


def local(
    layer_input,
    enc_weight,
    enc_bias,
    active,
    dec_weight,
    dec_bias,
    sae_error,
    positions,
    attn_gain,
    query_weight,
    kv_weight,
    out_weight,
    mlp_gain,
    gate_weight,
    up_weight,
    down_weight,
    cotangent,
):
    feat = lax.axis_index(FEAT)
    core = lax.axis_index("c")
    width = enc_weight.shape[1]
    hidden = gate_weight.shape[1]
    head_width = query_weight.shape[1]
    own_rows = POINTS * SEQ

    first_sums = jnp.concatenate(
        [dot(layer_input, enc_weight), dot_t(cotangent, down_weight)], axis=1
    )
    first_sums = tok_sums(first_sums)
    encoded = first_sums[:, :width]
    back_hidden = first_sums[:, width:]
    alphas = jnp.arange(1, POINTS + 1, dtype=F32) / POINTS
    features = active.reshape(POINTS, SEQ, width).astype(F32) * (
        alphas[:, None, None] * encoded[None] + enc_bias
    )
    sent_features = features.reshape(own_rows, width).astype(B16)
    decoded = feat_sums(dot(tok_rows_wide(sent_features, core), dec_weight))

    first_token = (feat // POINTS) * SEQ
    error_rows = lax.dynamic_slice_in_dim(sae_error, first_token, SEQ, 0).astype(F32)
    cot_rows = lax.dynamic_slice_in_dim(cotangent, first_token, SEQ, 0).astype(F32)
    hidden_in = decoded + dec_bias + error_rows

    gained = feat_rows((hidden_in * attn_gain).astype(B16))
    squares = jnp.sum(jnp.square(gained.astype(F32) * (1.0 / attn_gain)), axis=1, keepdims=True)
    qkv_weight = jnp.concatenate([query_weight, own_keyval_weight(kv_weight)], axis=1)
    projections = jnp.concatenate(
        [dot(gained, qkv_weight).astype(B16), split_column(squares)], axis=1
    )
    projections = tok_sums(projections)
    qkv_width = qkv_weight.shape[1]
    scale_rows = lax.rsqrt(joined_column(projections[:, qkv_width:]) / D + epsilon)
    query_rows = projections[:, :head_width] * scale_rows
    keyval_rows = (projections[:, head_width:qkv_width] * scale_rows).astype(B16).astype(F32)

    position_rows = jnp.broadcast_to(positions.reshape(1, SEQ), (POINTS, SEQ)).reshape(own_rows, 1)
    frequency = rope_base ** (-jnp.arange(HD // 2, dtype=F32) * 2.0 / HD)
    angles = position_rows.astype(F32) * frequency
    cosine, sine = jnp.cos(angles), jnp.sin(angles)
    heads = head_width // HD
    row_of = lax.broadcasted_iota(jnp.int32, (heads * own_rows, own_rows), 0) % own_rows
    key_of = lax.broadcasted_iota(jnp.int32, (heads * own_rows, own_rows), 1)
    visible = (row_of // SEQ == key_of // SEQ) & (row_of >= key_of)
    attended, pullback = jax.vjp(
        lambda left, right: attend(left, right, cosine, sine, visible), query_rows, keyval_rows
    )
    projected = feat_sums(dot(tok_rows(attended.astype(B16)), out_weight))
    middle = hidden_in + projected

    gained = feat_rows((middle * mlp_gain).astype(B16))
    squares = jnp.sum(jnp.square(gained.astype(F32) * (1.0 / mlp_gain)), axis=1, keepdims=True)
    gate_up = jnp.concatenate(
        [dot(gained, gate_weight), dot(gained, up_weight), split_column(squares).astype(F32)],
        axis=1,
    )
    gate_up = tok_sums_wide(gate_up, core)
    scale_mlp = lax.rsqrt(joined_column(gate_up[:, 2 * hidden :]) / D + epsilon)
    gate_value = gate_up[:, :hidden] * scale_mlp
    up_value = gate_up[:, hidden : 2 * hidden] * scale_mlp
    back_rows = jnp.broadcast_to(back_hidden[None], (POINTS, SEQ, hidden)).reshape(own_rows, hidden)
    sigmoid_gate = jax.nn.sigmoid(gate_value)
    grad_gate = back_rows * up_value * sigmoid_gate * (1.0 + gate_value * (1.0 - sigmoid_gate))
    grad_up = back_rows * gate_value * sigmoid_gate
    mlp_grads = jnp.concatenate(
        [grad_gate.astype(B16), grad_up.astype(B16), split_column(scale_rows), split_column(scale_mlp)],
        axis=1,
    )
    mlp_grads = tok_rows_wide(mlp_grads, core)
    back_second = feat_sums(
        dot_t(mlp_grads[:, :hidden], gate_weight) + dot_t(mlp_grads[:, hidden : 2 * hidden], up_weight)
    )
    scales = lax.dynamic_slice_in_dim(mlp_grads[:, 2 * hidden :], feat * SEQ, SEQ, 0)
    scale_first = joined_column(scales[:, :128])
    scale_second = joined_column(scales[:, 128:])

    weighted_second = back_second * mlp_gain
    grad_middle = (
        cot_rows
        + scale_second * weighted_second
        - middle * scale_second**3 * (row_total(weighted_second * middle) / D)
    )
    grad_attended = tok_sums(dot_t(feat_rows(grad_middle.astype(B16)), out_weight))
    grad_query, grad_keyval = pullback(grad_attended)
    attn_grads = jnp.concatenate([grad_query, grad_keyval], axis=1).astype(B16)
    back_first = feat_sums(dot_t(tok_rows(attn_grads), qkv_weight))
    weighted_first = back_first * attn_gain
    grad_hidden = (
        grad_middle
        + scale_first * weighted_first
        - hidden_in * scale_first**3 * (row_total(weighted_first * hidden_in) / D)
    )
    feature_grads = tok_sums_wide(dot_t(feat_rows(grad_hidden.astype(B16)), dec_weight), core)
    previous = jnp.concatenate([jnp.zeros_like(features[:1]), features[:-1]], axis=0)
    return jnp.sum(feature_grads.reshape(POINTS, SEQ, width) * (features - previous), axis=0)


def solution(mesh):
    fine = Mesh(mesh.devices.reshape(NY, NZ, NX, NC), FEAT + TOK)
    in_specs = (
        P(None, TOK),
        P(TOK, FEAT),
        P(FEAT),
        P(TOK, FEAT),
        P(FEAT, TOK),
        P(TOK),
        P(None, TOK),
        P(TOK, None),
        P(TOK),
        P(TOK, FEAT),
        P(TOK, FEAT),
        P(FEAT, TOK),
        P(TOK),
        P(TOK, FEAT),
        P(TOK, FEAT),
        P(FEAT, TOK),
        P(None, TOK),
    )
    return jax.shard_map(
        local, mesh=fine, in_specs=in_specs, out_specs=P(TOK, FEAT), check_vma=False
    )
```

```python
import jax
import jax.numpy as jnp
import numpy as np
from jax import lax
from jax.sharding import Mesh
from jax.sharding import PartitionSpec as P

D = 8192
HD = 128
POINTS = 4
SEQ = 16
NY, NZ, NX, NC = 4, 8, 4, 2
QUAD = 4
Z = ("half", "quad")
FEAT = ("y", "half", "quad")
TOK = ("x", "c")

epsilon = 1e-05
rope_base = 500000.0
F32 = jnp.float32
B16 = jnp.bfloat16


def dot(left_side, right_side):
    return jnp.dot(left_side, right_side, preferred_element_type=F32)


def dot_t(left_side, right_side):
    return lax.dot_general(
        left_side, right_side, (((1,), (1,)), ((), ())), preferred_element_type=F32
    )


def exact(left_side, right_side, left_dim, right_dim):
    return lax.dot_general(
        left_side,
        right_side,
        (((left_dim,), (right_dim,)), ((), ())),
        precision=lax.Precision.HIGHEST,
        preferred_element_type=F32,
    )


def swap(blocks, axes):
    return lax.all_to_all(blocks, axes, 0, 0, tiled=True)


def spread(piece, axes, count):
    blocks = jnp.broadcast_to(piece[None], (count,) + piece.shape)
    return swap(lax.optimization_barrier(blocks), axes).reshape((-1,) + piece.shape[1:])


def added(blocks):
    return jnp.sum(blocks.astype(F32), axis=0)


def feat_sums(partial):
    rows, width = partial.shape
    blocks = swap(partial.astype(B16).reshape(NY, rows // NY, width), "y")
    blocks = added(blocks).astype(B16).reshape(NZ, rows // (NY * NZ), width)
    return added(swap(blocks, Z))


def feat_rows(piece, first_core=None):
    piece = spread(piece, Z, NZ)
    if first_core is not None:
        halves = piece.reshape((2, -1) + piece.shape[1:])
        piece = jnp.where(first_core, halves, halves[::-1]).reshape(piece.shape)
    return spread(piece, "y", NY)


def tok_sums(partial):
    rows, width = partial.shape
    return added(swap(partial.astype(B16).reshape(NX * NC, rows // (NX * NC), width), TOK))


def other_core(values):
    return lax.ppermute(values, "c", [(0, 1), (1, 0)])


def tok_sums_core_first(rows, product):
    blocks = rows.reshape(NX, NC, -1, rows.shape[-1])
    height = blocks.shape[2]
    other = product(blocks[:, 1].reshape(NX * height, -1))
    received = other_core(other.astype(B16))
    own = product(blocks[:, 0].reshape(NX * height, -1))
    own = (own + received.astype(F32)).astype(B16)
    return added(swap(own.reshape(NX, height, -1), "x"))


def tok_rows(piece):
    return spread(piece, TOK, NX * NC)


def both_cores(own, first_core, piece):
    own = own.reshape((NX,) + piece.shape)
    other = other_core(own)
    first = jnp.where(first_core, own, other)
    second = jnp.where(first_core, other, own)
    return jnp.stack([first, second], axis=1).reshape((-1,) + piece.shape[1:])


def split_column(masks, *columns):
    block = jnp.zeros((columns[0].shape[0], 128), F32)
    for index, values in enumerate(columns):
        high = lax.reduce_precision(values, 8, 7)
        block = jnp.where(masks[2 * index], high, block)
        block = jnp.where(masks[2 * index + 1], values - high, block)
    return block.astype(B16)


def joined_column(block, first=0):
    return block[:, first : first + 1].astype(F32) + block[:, first + 1 : first + 2].astype(F32)


def rotate(vectors, cosine, sine):
    half = vectors.shape[-1] // 2
    first, second = vectors[:, :half], vectors[:, half:]
    return jnp.concatenate(
        [first * cosine - second * sine, second * cosine + first * sine], axis=-1
    )


def stacked_heads(values):
    heads = values.shape[1] // HD
    return jnp.concatenate([values[:, h * HD : (h + 1) * HD] for h in range(heads)], axis=0)


def side_by_side(values):
    heads = values.shape[0] // SEQ
    return jnp.concatenate([values[h * SEQ : (h + 1) * SEQ] for h in range(heads)], axis=1)


def attend(query_rows, keyval_rows, cosine, sine, visible):
    half = keyval_rows.shape[1] // 2
    tables = [
        jnp.concatenate([table] * (width // HD), axis=0)
        for width in (query_rows.shape[1], half)
        for table in (cosine, sine)
    ]
    queries = rotate(stacked_heads(query_rows), tables[0], tables[1])
    keys = rotate(stacked_heads(keyval_rows[:, :half]), tables[2], tables[3])
    values = stacked_heads(keyval_rows[:, half:])
    scores = exact(queries, keys, 1, 1) * HD ** (-0.5)
    scores = jnp.where(visible, scores, -1e30)
    weights = jnp.exp(scores - jnp.max(scores, axis=-1, keepdims=True))
    weights = weights / jnp.sum(weights, axis=-1, keepdims=True)
    saved = (queries, keys, values, weights, tables)
    return side_by_side(exact(weights, values, 1, 0)), saved


def attend_back(grad_attended, saved):
    queries, keys, values, weights, tables = saved
    grads = stacked_heads(grad_attended)
    grad_values = exact(weights, grads, 0, 0)
    grad_weights = exact(grads, values, 1, 1)
    mean_grad = jnp.sum(grad_weights * weights, axis=-1, keepdims=True)
    grad_scores = weights * (grad_weights - mean_grad) * HD ** (-0.5)
    grad_queries = rotate(exact(grad_scores, keys, 1, 0), tables[0], -tables[1])
    grad_keys = rotate(exact(grad_scores, queries, 0, 0), tables[2], -tables[3])
    return side_by_side(grad_queries), jnp.concatenate(
        [side_by_side(grad_keys), side_by_side(grad_values)], axis=1
    )


def turned(weight):
    return dot_t(jnp.eye(weight.shape[1], dtype=B16), weight).astype(B16)


def placed_block(block):
    moves = []
    for source in range(NY * NZ):
        row, place = divmod(source, NZ)
        half = (place // 2) % 2
        moves.append((source, NZ * row + QUAD * half + 2 * (place // QUAD) + place % 2))
    return lax.ppermute(block, FEAT, moves)


def prepared(attn_gain, mlp_gain, sae_error, cotangent):
    feat = lax.axis_index(FEAT)
    first_token = (feat // POINTS) * SEQ
    row = np.arange(NZ * SEQ)
    key = np.arange(NY * SEQ)
    visible = (row[:, None] // (2 * SEQ) == key // SEQ) & (row[:, None] % SEQ >= key % SEQ)
    return dict(
        own_prompt=2 * lax.axis_index("y") + lax.axis_index(TOK) // POINTS,
        first_core=lax.axis_index("c") == 0,
        visible=jnp.asarray(visible),
        masks=[jnp.asarray(np.arange(128)[None, :] == lane) for lane in range(6)],
        attn_unscaled=1.0 / attn_gain,
        mlp_unscaled=1.0 / mlp_gain,
        error_rows=lax.dynamic_slice_in_dim(sae_error, first_token, SEQ, 0).astype(F32),
        cot_rows=lax.dynamic_slice_in_dim(cotangent, first_token, SEQ, 0).astype(F32),
    )


def feat_part_rows(piece):
    return spread(piece, Z, NZ)


def feat_part_sums(partial):
    rows, width = partial.shape
    return added(swap(partial.astype(B16).reshape(NZ, rows // NZ, width), Z))


def local(
    layer_input,
    enc_weight,
    enc_bias,
    active,
    dec_weight,
    dec_bias,
    sae_error,
    positions,
    attn_gain,
    query_weight,
    kv_weight,
    out_weight,
    mlp_gain,
    gate_weight,
    up_weight,
    down_weight,
    cotangent,
):
    width = enc_weight.shape[1]
    hidden = gate_weight.shape[1]
    model_width = dec_weight.shape[1]

    first_sums = jnp.concatenate(
        [dot(layer_input, enc_weight).astype(B16), dot_t(cotangent, down_weight).astype(B16)],
        axis=1,
    ).reshape(NX * NC, SEQ, width + hidden)
    own_positions = jnp.broadcast_to(
        positions.reshape(1, SEQ, 1).astype(B16), (NX * NC, SEQ, 128)
    )
    blocks = swap(jnp.concatenate([first_sums, own_positions], axis=2), TOK)
    ready = prepared(attn_gain, mlp_gain, sae_error, cotangent)
    active_rows = active.reshape(POINTS, SEQ, width).astype(F32)
    turned_rows = jnp.concatenate(
        [turned(query_weight), placed_block(turned(kv_weight))], axis=0
    )
    turned_rows = lax.all_gather(turned_rows, "y", axis=0, tiled=True)
    blocks, ready, active_rows, gate_weight, up_weight = lax.optimization_barrier(
        (blocks, ready, active_rows, gate_weight, up_weight)
    )
    first_core, masks = ready["first_core"], ready["masks"]
    first_sums = added(blocks[:, :, : width + hidden])
    own_positions = lax.dynamic_index_in_dim(
        blocks[:, :, width + hidden], ready["own_prompt"], 0, keepdims=False
    ).astype(F32)
    frequency = (rope_base ** (-np.arange(HD // 2) * 2.0 / HD)).astype(np.float32)
    angles = own_positions[:, None] * frequency
    cosine, sine = jnp.cos(angles), jnp.sin(angles)
    encoded = first_sums[:, :width]
    back_hidden = first_sums[:, width:]
    features = [
        active_rows[k] * ((k + 1) / POINTS * encoded + enc_bias) for k in range(POINTS)
    ]
    changes = [features[0]] + [features[k] - features[k - 1] for k in range(1, POINTS)]
    changes = jnp.concatenate(changes, axis=0)
    sent_features = jnp.concatenate(features, axis=0).astype(B16)
    own_rows = spread(sent_features, "x", NX)
    back_rows = jnp.concatenate([back_hidden] * POINTS, axis=0)
    gate_up_weight = jnp.concatenate([gate_weight, up_weight], axis=1)
    own_rows, changes, back_rows, gate_up_weight, cosine, sine = lax.optimization_barrier(
        (own_rows, changes, back_rows, gate_up_weight, cosine, sine)
    )
    gathered = both_cores(own_rows, first_core, sent_features)
    decoded = feat_sums(dot(gathered, dec_weight))
    out_rows = lax.all_gather(out_weight, "y", axis=0, tiled=True)
    hidden_in = decoded + dec_bias + ready["error_rows"]

    gained = feat_part_rows((hidden_in * attn_gain).astype(B16))
    squares = jnp.sum(
        jnp.square(gained.astype(F32) * ready["attn_unscaled"]), axis=1, keepdims=True
    )
    projections = tok_sums(
        jnp.concatenate(
            [dot_t(gained, turned_rows).astype(B16), split_column(masks, squares)], axis=1
        )
    )
    projections, out_rows = lax.optimization_barrier((projections, out_rows))
    head_part = query_weight.shape[1]
    qkv_width = turned_rows.shape[0]
    scale_rows = lax.rsqrt(joined_column(projections[:, qkv_width:]) / D + epsilon)
    own_qkv = (projections[:, :qkv_width] * scale_rows).reshape(SEQ, NY, qkv_width // NY)
    kv_part = own_qkv.shape[2] - head_part
    own_keyval = own_qkv[:, :, head_part:].astype(B16).reshape(SEQ, NY * kv_part)
    keyval = spread(own_keyval, "quad", QUAD).reshape(QUAD, SEQ, NY, kv_part)
    attended, saved = attend(
        own_qkv[:, :, :head_part].reshape(SEQ, -1),
        keyval.transpose(1, 2, 0, 3).reshape(SEQ, -1).astype(F32),
        cosine,
        sine,
        ready["visible"],
    )
    attended, saved = lax.optimization_barrier((attended.astype(B16), saved))
    projected = feat_part_sums(dot(tok_rows(attended), out_rows))
    middle = hidden_in + projected

    gained = feat_rows((middle * mlp_gain).astype(B16), first_core)

    def gate_up_product(rows):
        squares = jnp.sum(
            jnp.square(rows.astype(F32) * ready["mlp_unscaled"]), axis=1, keepdims=True
        )
        return jnp.concatenate(
            [dot(rows, gate_up_weight).astype(B16), split_column(masks, squares)], axis=1
        ).astype(F32)

    gate_up = tok_sums_core_first(gained, gate_up_product)
    scale_mlp = lax.rsqrt(joined_column(gate_up[:, 2 * hidden :]) / D + epsilon)
    gate_raw = gate_up[:, :hidden]
    up_raw = gate_up[:, hidden : 2 * hidden]
    gate_value = gate_raw * scale_mlp
    up_value = up_raw * scale_mlp
    sigmoid_gate = jax.nn.sigmoid(gate_value)
    grad_gate = back_rows * up_value * sigmoid_gate * (1.0 + gate_value * (1.0 - sigmoid_gate))
    grad_up = back_rows * gate_value * sigmoid_gate
    grad_gate, grad_up = grad_gate.astype(B16), grad_up.astype(B16)
    meeting = jnp.sum(
        grad_gate.astype(F32) * gate_raw + grad_up.astype(F32) * up_raw, axis=1, keepdims=True
    )
    mlp_grads = jnp.concatenate(
        [grad_gate, grad_up, split_column(masks, scale_mlp, meeting)], axis=1
    )
    mlp_grads = both_cores(spread(mlp_grads, "x", NX), first_core, mlp_grads)
    back_second = feat_sums(
        jnp.concatenate(
            [
                dot_t(mlp_grads[:, : 2 * hidden], gate_up_weight).astype(B16),
                mlp_grads[:, 2 * hidden :],
            ],
            axis=1,
        )
    )
    extras = back_second[:, model_width:]
    scale_second = joined_column(extras) / (NY * NZ)
    total = joined_column(extras, 2)
    weighted_second = back_second[:, :model_width] * mlp_gain
    grad_middle = (
        ready["cot_rows"]
        + scale_second * weighted_second
        - middle * scale_second**3 * (total / D)
    )
    gathered = feat_part_rows(grad_middle.astype(B16))
    grad_attended = tok_sums(dot_t(gathered, out_rows))
    grad_query, grad_keyval = attend_back(grad_attended, saved)
    grad_keyval = grad_keyval.astype(B16).reshape(SEQ, NY, QUAD, kv_part)
    grad_keyval = added(swap(grad_keyval.transpose(2, 0, 1, 3).reshape(QUAD, SEQ, -1), "quad"))
    attn_grads = jnp.concatenate(
        [grad_query.reshape(SEQ, NY, head_part), grad_keyval.reshape(SEQ, NY, kv_part)], axis=2
    )
    attn_grads = attn_grads.reshape(SEQ, qkv_width).astype(B16)
    meeting = jnp.sum(
        attn_grads.astype(F32) * projections[:, :qkv_width], axis=1, keepdims=True
    )
    gathered = tok_rows(
        jnp.concatenate([attn_grads, split_column(masks, meeting, scale_rows)], axis=1)
    )
    back_first = feat_part_sums(
        jnp.concatenate(
            [
                dot(gathered[:, :qkv_width], turned_rows).astype(B16),
                gathered[:, qkv_width:],
            ],
            axis=1,
        )
    )
    extras = back_first[:, model_width:]
    total = joined_column(extras)
    scale_first = joined_column(extras, 2) / NZ
    weighted_first = back_first[:, :model_width] * attn_gain
    grad_hidden = (
        grad_middle
        + scale_first * weighted_first
        - hidden_in * scale_first**3 * (total / D)
    )
    gathered = feat_rows(grad_hidden.astype(B16), first_core)
    feature_grads = tok_sums_core_first(gathered, lambda rows: dot_t(rows, dec_weight))
    return jnp.sum((feature_grads * changes).reshape(POINTS, SEQ, width), axis=0)


def solution(mesh):
    fine = Mesh(mesh.devices.reshape(NY, NZ // QUAD, QUAD, NX, NC), FEAT + TOK)
    in_specs = (
        P(None, TOK),
        P(TOK, FEAT),
        P(FEAT),
        P(TOK, FEAT),
        P(FEAT, TOK),
        P(TOK),
        P(None, TOK),
        P(TOK, None),
        P(TOK),
        P(TOK, FEAT),
        P(TOK, FEAT),
        P(FEAT, TOK),
        P(TOK),
        P(TOK, FEAT),
        P(TOK, FEAT),
        P(FEAT, TOK),
        P(None, TOK),
    )
    return jax.shard_map(
        local, mesh=fine, in_specs=in_specs, out_specs=P(TOK, FEAT), check_vma=False
    )
```

```python
import jax
import jax.numpy as jnp
import numpy as np
from jax import lax
from jax.sharding import Mesh
from jax.sharding import PartitionSpec as P

D = 8192
HD = 128
POINTS = 4
SEQ = 16
NY, NZ, NX, NC = 4, 8, 4, 2
QUAD = 4
Z = ("half", "quad")
FEAT = ("y", "half", "quad")
TOK = ("x", "c")

epsilon = 1e-05
rope_base = 500000.0
F32 = jnp.float32
B16 = jnp.bfloat16


def dot(left_side, right_side):
    return jnp.dot(left_side, right_side, preferred_element_type=F32)


def dot_t(left_side, right_side):
    return lax.dot_general(
        left_side, right_side, (((1,), (1,)), ((), ())), preferred_element_type=F32
    )


def exact(left_side, right_side, left_dim, right_dim):
    return lax.dot_general(
        left_side,
        right_side,
        (((left_dim,), (right_dim,)), ((), ())),
        precision=lax.Precision.HIGHEST,
        preferred_element_type=F32,
    )


def swap(blocks, axes):
    return lax.all_to_all(blocks, axes, 0, 0, tiled=True)


def spread(piece, axes, count):
    blocks = jnp.broadcast_to(piece[None], (count,) + piece.shape)
    return swap(lax.optimization_barrier(blocks), axes).reshape((-1,) + piece.shape[1:])


def added(blocks):
    return jnp.sum(blocks.astype(F32), axis=0)


def feat_sums(partial):
    rows, width = partial.shape
    blocks = swap(partial.astype(B16).reshape(NY, rows // NY, width), "y")
    blocks = added(blocks).astype(B16).reshape(NZ, rows // (NY * NZ), width)
    return added(swap(blocks, Z))


def feat_rows(piece, first_core=None):
    piece = spread(piece, Z, NZ)
    if first_core is not None:
        halves = piece.reshape((2, -1) + piece.shape[1:])
        piece = jnp.where(first_core, halves, halves[::-1]).reshape(piece.shape)
    return spread(piece, "y", NY)


def tok_sums(partial):
    rows, width = partial.shape
    return added(swap(partial.astype(B16).reshape(NX * NC, rows // (NX * NC), width), TOK))


def other_core(values):
    return lax.ppermute(values, "c", [(0, 1), (1, 0)])


def tok_sums_core_first(rows, product):
    blocks = rows.reshape(NX, NC, -1, rows.shape[-1])
    height = blocks.shape[2]
    if height == SEQ:
        sums = product(rows).astype(B16).reshape(NX, NC, height, -1)
        own, other = sums[:, 0], sums[:, 1]
    else:
        other = product(blocks[:, 1].reshape(NX * height, -1)).astype(B16)
        own = product(blocks[:, 0].reshape(NX * height, -1))
    received = other_core(other).astype(F32).reshape(NX, height, -1)
    own = (own.astype(F32).reshape(NX, height, -1) + received).astype(B16)
    return added(swap(own, "x"))


def tok_rows(piece):
    return spread(piece, TOK, NX * NC)


def both_cores(own, first_core, piece):
    own = own.reshape((NX,) + piece.shape)
    other = other_core(own)
    first = jnp.where(first_core, own, other)
    second = jnp.where(first_core, other, own)
    return jnp.stack([first, second], axis=1).reshape((-1,) + piece.shape[1:])


def split_column(masks, *columns):
    block = jnp.zeros((columns[0].shape[0], 128), F32)
    for index, values in enumerate(columns):
        high = lax.reduce_precision(values, 8, 7)
        block = jnp.where(masks[2 * index], high, block)
        block = jnp.where(masks[2 * index + 1], values - high, block)
    return block.astype(B16)


def joined_column(block, first=0):
    return block[:, first : first + 1].astype(F32) + block[:, first + 1 : first + 2].astype(F32)


def rotate(vectors, cosine, sine):
    half = vectors.shape[-1] // 2
    first, second = vectors[:, :half], vectors[:, half:]
    return jnp.concatenate(
        [first * cosine - second * sine, second * cosine + first * sine], axis=-1
    )


def stacked_heads(values):
    heads = values.shape[1] // HD
    return jnp.concatenate([values[:, h * HD : (h + 1) * HD] for h in range(heads)], axis=0)


def side_by_side(values):
    heads = values.shape[0] // SEQ
    return jnp.concatenate([values[h * SEQ : (h + 1) * SEQ] for h in range(heads)], axis=1)


def attend(query_rows, keyval_rows, tables, visible):
    half = keyval_rows.shape[1] // 2
    queries = rotate(stacked_heads(query_rows), tables[0], tables[1])
    keys = rotate(stacked_heads(keyval_rows[:, :half]), tables[2], tables[3])
    values = stacked_heads(keyval_rows[:, half:])
    scores = exact(queries, keys, 1, 1) * HD ** (-0.5)
    scores = jnp.where(visible, scores, -1e30)
    weights = jnp.exp(scores - jnp.max(scores, axis=-1, keepdims=True))
    weights = weights / jnp.sum(weights, axis=-1, keepdims=True)
    saved = (queries, keys, values, weights, tables)
    return side_by_side(exact(weights, values, 1, 0)), saved


def attend_back(grad_attended, saved):
    queries, keys, values, weights, tables = saved
    grads = stacked_heads(grad_attended)
    grad_values = exact(weights, grads, 0, 0)
    grad_weights = exact(grads, values, 1, 1)
    mean_grad = jnp.sum(grad_weights * weights, axis=-1, keepdims=True)
    grad_scores = weights * (grad_weights - mean_grad) * HD ** (-0.5)
    grad_queries = rotate(exact(grad_scores, keys, 1, 0), tables[0], -tables[1])
    grad_keys = rotate(exact(grad_scores, queries, 0, 0), tables[2], -tables[3])
    return side_by_side(grad_queries), jnp.concatenate(
        [side_by_side(grad_keys), side_by_side(grad_values)], axis=1
    )


def turned(weight):
    return dot_t(jnp.eye(weight.shape[1], dtype=B16), weight).astype(B16)


def placed_block(block):
    moves = []
    for source in range(NY * NZ):
        row, place = divmod(source, NZ)
        half = (place // 2) % 2
        moves.append((source, NZ * row + QUAD * half + 2 * (place // QUAD) + place % 2))
    return lax.ppermute(block, FEAT, moves)


def prepared(attn_gain, mlp_gain, sae_error, cotangent):
    feat = lax.axis_index(FEAT)
    first_token = (feat // POINTS) * SEQ
    row = np.arange(NZ * SEQ)
    key = np.arange(NY * SEQ)
    visible = (row[:, None] // (2 * SEQ) == key // SEQ) & (row[:, None] % SEQ >= key % SEQ)
    return dict(
        own_prompt=2 * lax.axis_index("y") + lax.axis_index(TOK) // POINTS,
        late_prompt=lax.axis_index(TOK) // POINTS == 1,
        first_core=lax.axis_index("c") == 0,
        visible=jnp.asarray(visible),
        masks=[jnp.asarray(np.arange(128)[None, :] == lane) for lane in range(6)],
        attn_unscaled=1.0 / attn_gain,
        mlp_unscaled=1.0 / mlp_gain,
        error_rows=lax.dynamic_slice_in_dim(sae_error, first_token, SEQ, 0).astype(F32),
        cot_rows=lax.dynamic_slice_in_dim(cotangent, first_token, SEQ, 0).astype(F32),
    )


def feat_part_rows(piece):
    return spread(piece, Z, NZ)


def feat_part_sums(partial):
    rows, width = partial.shape
    return added(swap(partial.astype(B16).reshape(NZ, rows // NZ, width), Z))


def local(
    layer_input,
    enc_weight,
    enc_bias,
    active,
    dec_weight,
    dec_bias,
    sae_error,
    positions,
    attn_gain,
    query_weight,
    kv_weight,
    out_weight,
    mlp_gain,
    gate_weight,
    up_weight,
    down_weight,
    cotangent,
):
    width = enc_weight.shape[1]
    hidden = gate_weight.shape[1]
    model_width = dec_weight.shape[1]

    first_sums = jnp.concatenate(
        [dot(layer_input, enc_weight).astype(B16), dot_t(cotangent, down_weight).astype(B16)],
        axis=1,
    ).reshape(NX * NC, SEQ, width + hidden)
    own_positions = jnp.broadcast_to(
        positions.reshape(1, SEQ, 1).astype(B16), (NX * NC, SEQ, 128)
    )
    blocks = swap(jnp.concatenate([first_sums, own_positions], axis=2), TOK)
    ready = prepared(attn_gain, mlp_gain, sae_error, cotangent)
    active_rows = active.reshape(POINTS, SEQ, width).astype(F32)
    turned_rows = jnp.concatenate(
        [turned(query_weight), placed_block(turned(kv_weight))], axis=0
    )
    turned_rows = lax.all_gather(turned_rows, "y", axis=0, tiled=True)
    blocks, ready, active_rows, gate_weight, up_weight = lax.optimization_barrier(
        (blocks, ready, active_rows, gate_weight, up_weight)
    )
    first_core, masks = ready["first_core"], ready["masks"]
    first_sums = added(blocks[:, :, : width + hidden])
    own_positions = lax.dynamic_index_in_dim(
        blocks[:, :, width + hidden], ready["own_prompt"], 0, keepdims=False
    ).astype(F32)
    frequency = (rope_base ** (-np.arange(HD // 2) * 2.0 / HD)).astype(np.float32)
    angles = own_positions[:, None] * frequency
    tables = [
        jnp.concatenate([table] * count, axis=0)
        for count in (NZ, NY)
        for table in (jnp.cos(angles), jnp.sin(angles))
    ]
    encoded = first_sums[:, :width]
    back_hidden = first_sums[:, width:]
    features = [
        active_rows[k] * ((k + 1) / POINTS * encoded + enc_bias) for k in range(POINTS)
    ]
    changes = [features[0]] + [features[k] - features[k - 1] for k in range(1, POINTS)]
    changes = jnp.concatenate(changes, axis=0)
    sent_rows = jnp.concatenate(
        features + [back_hidden.reshape(-1, width)], axis=0
    ).astype(B16)
    feature_rows = POINTS * SEQ
    own_rows = spread(sent_rows, "x", NX)
    gate_up_turned = jnp.concatenate([turned(gate_weight), turned(up_weight)], axis=0)
    own_rows, changes, gate_up_turned, tables = lax.optimization_barrier(
        (own_rows, changes, gate_up_turned, tables)
    )
    gathered = both_cores(own_rows, first_core, sent_rows).reshape((NX * NC,) + sent_rows.shape)
    features = gathered[:, :feature_rows].reshape(-1, width)
    back_hidden = gathered[:, feature_rows:].reshape(NY, -1, width)
    decoded = dot(features, dec_weight).astype(B16).reshape(NY, -1, model_width)
    blocks = swap(jnp.concatenate([decoded, back_hidden], axis=1), "y")
    chunk_rows = decoded.shape[1]
    back_hidden = blocks[:, chunk_rows:].reshape(NY, 2, SEQ, hidden)
    back_hidden = jnp.where(ready["late_prompt"], back_hidden[:, 1], back_hidden[:, 0])
    back_hidden = back_hidden.transpose(1, 0, 2).astype(F32)
    decoded = added(blocks[:, :chunk_rows]).astype(B16).reshape(NZ, SEQ, model_width)
    decoded, back_hidden = lax.optimization_barrier((decoded, back_hidden))
    decoded = added(swap(decoded, Z))
    out_rows = lax.all_gather(out_weight, "y", axis=0, tiled=True)
    decoded, gate_up_turned = lax.optimization_barrier((decoded, gate_up_turned))
    gate_up_turned = lax.all_gather(gate_up_turned, "y", axis=0, tiled=True)
    hidden_in = decoded + dec_bias + ready["error_rows"]

    gained = feat_part_rows((hidden_in * attn_gain).astype(B16))
    squares = jnp.sum(
        jnp.square(gained.astype(F32) * ready["attn_unscaled"]), axis=1, keepdims=True
    )
    projections = tok_sums(
        jnp.concatenate(
            [dot_t(gained, turned_rows).astype(B16), split_column(masks, squares)], axis=1
        )
    )
    projections, out_rows = lax.optimization_barrier((projections, out_rows))
    head_part = query_weight.shape[1]
    qkv_width = turned_rows.shape[0]
    scale_rows = lax.rsqrt(joined_column(projections[:, qkv_width:]) / D + epsilon)
    own_qkv = (projections[:, :qkv_width] * scale_rows).reshape(SEQ, NY, qkv_width // NY)
    kv_part = own_qkv.shape[2] - head_part
    own_keyval = own_qkv[:, :, head_part:].astype(B16).reshape(SEQ, NY * kv_part)
    keyval = spread(own_keyval, "quad", QUAD).reshape(QUAD, SEQ, NY, kv_part)
    attended, saved = attend(
        own_qkv[:, :, :head_part].reshape(SEQ, -1),
        keyval.transpose(1, 2, 0, 3).reshape(SEQ, -1).astype(F32),
        tables,
        ready["visible"],
    )
    attended, saved = lax.optimization_barrier((attended.astype(B16), saved))
    projected = feat_part_sums(dot(tok_rows(attended), out_rows))
    middle = hidden_in + projected

    gained = feat_part_rows((middle * mlp_gain).astype(B16))
    gained = gained.reshape(NX, NC, SEQ, model_width)
    gained = jnp.where(first_core, gained, gained[:, ::-1])

    def gate_up_product(rows):
        squares = jnp.sum(
            jnp.square(rows.astype(F32) * ready["mlp_unscaled"]), axis=1, keepdims=True
        )
        return jnp.concatenate(
            [dot_t(rows, gate_up_turned).astype(B16), split_column(masks, squares)], axis=1
        ).astype(F32)

    gate_up = tok_sums_core_first(gained.reshape(-1, model_width), gate_up_product)
    scale_mlp = lax.rsqrt(joined_column(gate_up[:, NY * 2 * hidden :]) / D + epsilon)
    gate_up = gate_up[:, : NY * 2 * hidden].reshape(SEQ, NY, 2 * hidden)
    gate_raw = gate_up[:, :, :hidden]
    up_raw = gate_up[:, :, hidden:]
    gate_value = gate_raw * scale_mlp[:, :, None]
    up_value = up_raw * scale_mlp[:, :, None]
    sigmoid_gate = jax.nn.sigmoid(gate_value)
    grad_gate = back_hidden * up_value * sigmoid_gate * (1.0 + gate_value * (1.0 - sigmoid_gate))
    grad_up = back_hidden * gate_value * sigmoid_gate
    grad_gate, grad_up = grad_gate.astype(B16), grad_up.astype(B16)
    meeting = jnp.sum(
        grad_gate.astype(F32) * gate_raw + grad_up.astype(F32) * up_raw, axis=(1, 2)
    )[:, None]
    mlp_grads = jnp.concatenate([grad_gate, grad_up], axis=2).reshape(SEQ, -1)
    mlp_grads = jnp.concatenate([mlp_grads, split_column(masks, scale_mlp, meeting)], axis=1)
    mlp_grads = both_cores(spread(mlp_grads, "x", NX), first_core, mlp_grads)
    mlp_width = NY * 2 * hidden
    back_second = feat_part_sums(
        jnp.concatenate(
            [
                dot(mlp_grads[:, :mlp_width], gate_up_turned).astype(B16),
                mlp_grads[:, mlp_width:],
            ],
            axis=1,
        )
    )
    extras = back_second[:, model_width:]
    scale_second = joined_column(extras) / NZ
    total = joined_column(extras, 2)

    weighted_second = back_second[:, :model_width] * mlp_gain
    grad_middle = (
        ready["cot_rows"]
        + scale_second * weighted_second
        - middle * scale_second**3 * (total / D)
    )
    gathered = feat_part_rows(grad_middle.astype(B16))
    grad_attended = tok_sums(dot_t(gathered, out_rows))
    grad_query, grad_keyval = attend_back(grad_attended, saved)
    grad_keyval = grad_keyval.astype(B16).reshape(SEQ, NY, QUAD, kv_part)
    grad_keyval = added(swap(grad_keyval.transpose(2, 0, 1, 3).reshape(QUAD, SEQ, -1), "quad"))
    attn_grads = jnp.concatenate(
        [grad_query.reshape(SEQ, NY, head_part), grad_keyval.reshape(SEQ, NY, kv_part)], axis=2
    )
    attn_grads = attn_grads.reshape(SEQ, qkv_width).astype(B16)
    meeting = jnp.sum(
        attn_grads.astype(F32) * projections[:, :qkv_width], axis=1, keepdims=True
    )
    gathered = tok_rows(
        jnp.concatenate([attn_grads, split_column(masks, meeting, scale_rows)], axis=1)
    )
    back_first = feat_part_sums(
        jnp.concatenate(
            [
                dot(gathered[:, :qkv_width], turned_rows).astype(B16),
                gathered[:, qkv_width:],
            ],
            axis=1,
        )
    )
    extras = back_first[:, model_width:]
    total = joined_column(extras)
    scale_first = joined_column(extras, 2) / NZ
    weighted_first = back_first[:, :model_width] * attn_gain
    grad_hidden = (
        grad_middle
        + scale_first * weighted_first
        - hidden_in * scale_first**3 * (total / D)
    )
    gathered = feat_rows(grad_hidden.astype(B16), first_core)
    feature_grads = tok_sums_core_first(gathered, lambda rows: dot_t(rows, dec_weight))
    return jnp.sum((feature_grads * changes).reshape(POINTS, SEQ, width), axis=0)


def solution(mesh):
    fine = Mesh(mesh.devices.reshape(NY, NZ // QUAD, QUAD, NX, NC), FEAT + TOK)
    in_specs = (
        P(None, TOK),
        P(TOK, FEAT),
        P(FEAT),
        P(TOK, FEAT),
        P(FEAT, TOK),
        P(TOK),
        P(None, TOK),
        P(TOK, None),
        P(TOK),
        P(TOK, FEAT),
        P(TOK, FEAT),
        P(FEAT, TOK),
        P(TOK),
        P(TOK, FEAT),
        P(TOK, FEAT),
        P(FEAT, TOK),
        P(None, TOK),
    )
    return jax.shard_map(
        local, mesh=fine, in_specs=in_specs, out_specs=P(TOK, FEAT), check_vma=False
    )
```

```python
import jax
import jax.numpy as jnp
import numpy as np
from jax import lax
from jax.sharding import Mesh
from jax.sharding import PartitionSpec as P

D = 8192
HD = 128
POINTS = 4
SEQ = 16
NY, NZ, NX, NC = 4, 8, 4, 2
QUAD = 4
Z = ("half", "quad")
FEAT = ("y", "half", "quad")
TOK = ("x", "c")

epsilon = 1e-05
rope_base = 500000.0
F32 = jnp.float32
B16 = jnp.bfloat16


def dot(left_side, right_side):
    return jnp.dot(left_side, right_side, preferred_element_type=F32)


def dot_t(left_side, right_side):
    return lax.dot_general(
        left_side, right_side, (((1,), (1,)), ((), ())), preferred_element_type=F32
    )


def exact(left_side, right_side, left_dim, right_dim):
    return lax.dot_general(
        left_side,
        right_side,
        (((left_dim,), (right_dim,)), ((), ())),
        precision=lax.Precision.HIGHEST,
        preferred_element_type=F32,
    )


def swap(blocks, axes):
    return lax.all_to_all(blocks, axes, 0, 0, tiled=True)


def spread(piece, axes, count):
    blocks = jnp.broadcast_to(piece[None], (count,) + piece.shape)
    return swap(lax.optimization_barrier(blocks), axes).reshape((-1,) + piece.shape[1:])


def added(blocks):
    return jnp.sum(blocks.astype(F32), axis=0)


def feat_sums(partial):
    rows, width = partial.shape
    blocks = swap(partial.astype(B16).reshape(NY, rows // NY, width), "y")
    blocks = added(blocks).astype(B16).reshape(NZ, rows // (NY * NZ), width)
    return added(swap(blocks, Z))


def feat_rows(piece, first_core=None):
    piece = spread(piece, Z, NZ)
    if first_core is not None:
        halves = piece.reshape((2, -1) + piece.shape[1:])
        piece = jnp.where(first_core, halves, halves[::-1]).reshape(piece.shape)
    return spread(piece, "y", NY)


def tok_sums(partial):
    rows, width = partial.shape
    return added(swap(partial.astype(B16).reshape(NX * NC, rows // (NX * NC), width), TOK))


def other_core(values):
    return lax.ppermute(values, "c", [(0, 1), (1, 0)])


def tok_sums_core_first(rows, product):
    blocks = rows.reshape(NX, NC, -1, rows.shape[-1])
    height = blocks.shape[2]
    if height == SEQ:
        sums = product(rows).astype(B16).reshape(NX, NC, height, -1)
        own, other = sums[:, 0], sums[:, 1]
    else:
        other = product(blocks[:, 1].reshape(NX * height, -1)).astype(B16)
        own = product(blocks[:, 0].reshape(NX * height, -1))
    received = other_core(other).astype(F32).reshape(NX, height, -1)
    own = (own.astype(F32).reshape(NX, height, -1) + received).astype(B16)
    return added(swap(own, "x"))


def tok_rows(piece):
    return spread(piece, TOK, NX * NC)


def both_cores(own, first_core, piece):
    own = own.reshape((NX,) + piece.shape)
    other = other_core(own)
    first = jnp.where(first_core, own, other)
    second = jnp.where(first_core, other, own)
    return jnp.stack([first, second], axis=1).reshape((-1,) + piece.shape[1:])


def split_column(masks, *columns):
    block = jnp.zeros((columns[0].shape[0], 128), F32)
    for index, values in enumerate(columns):
        high = lax.reduce_precision(values, 8, 7)
        block = jnp.where(masks[2 * index], high, block)
        block = jnp.where(masks[2 * index + 1], values - high, block)
    return block.astype(B16)


def joined_column(block, first=0):
    return block[:, first : first + 1].astype(F32) + block[:, first + 1 : first + 2].astype(F32)


def rotate(vectors, cosine, sine):
    half = vectors.shape[-1] // 2
    first, second = vectors[:, :half], vectors[:, half:]
    return jnp.concatenate(
        [first * cosine - second * sine, second * cosine + first * sine], axis=-1
    )


def stacked_heads(values):
    heads = values.shape[1] // HD
    return jnp.concatenate([values[:, h * HD : (h + 1) * HD] for h in range(heads)], axis=0)


def side_by_side(values):
    heads = values.shape[0] // SEQ
    return jnp.concatenate([values[h * SEQ : (h + 1) * SEQ] for h in range(heads)], axis=1)


def attend(query_rows, keyval_rows, tables, visible):
    half = keyval_rows.shape[1] // 2
    queries = rotate(stacked_heads(query_rows), tables[0], tables[1])
    keys = rotate(stacked_heads(keyval_rows[:, :half]), tables[2], tables[3])
    values = stacked_heads(keyval_rows[:, half:])
    scores = exact(queries, keys, 1, 1) * HD ** (-0.5)
    scores = jnp.where(visible, scores, -1e30)
    weights = jnp.exp(scores - jnp.max(scores, axis=-1, keepdims=True))
    weights = weights / jnp.sum(weights, axis=-1, keepdims=True)
    saved = (queries, keys, values, weights, tables)
    return side_by_side(exact(weights, values, 1, 0)), saved


def attend_back(grad_attended, saved):
    queries, keys, values, weights, tables = saved
    grads = stacked_heads(grad_attended)
    grad_values = exact(weights, grads, 0, 0)
    grad_weights = exact(grads, values, 1, 1)
    mean_grad = jnp.sum(grad_weights * weights, axis=-1, keepdims=True)
    grad_scores = weights * (grad_weights - mean_grad) * HD ** (-0.5)
    grad_queries = rotate(exact(grad_scores, keys, 1, 0), tables[0], -tables[1])
    grad_keys = rotate(exact(grad_scores, queries, 0, 0), tables[2], -tables[3])
    return side_by_side(grad_queries), jnp.concatenate(
        [side_by_side(grad_keys), side_by_side(grad_values)], axis=1
    )


def turned(weight):
    return dot_t(jnp.eye(weight.shape[1], dtype=B16), weight).astype(B16)


def placed_block(block):
    moves = []
    for source in range(NY * NZ):
        row, place = divmod(source, NZ)
        half = (place // 2) % 2
        moves.append((source, NZ * row + QUAD * half + 2 * (place // QUAD) + place % 2))
    return lax.ppermute(block, FEAT, moves)


def prepared(attn_gain, mlp_gain, sae_error, cotangent):
    feat = lax.axis_index(FEAT)
    first_token = (feat // POINTS) * SEQ
    row = np.arange(NZ * SEQ)
    key = np.arange(NY * SEQ)
    visible = (row[:, None] // (2 * SEQ) == key // SEQ) & (row[:, None] % SEQ >= key % SEQ)
    return dict(
        own_prompt=2 * lax.axis_index("y") + lax.axis_index(TOK) // POINTS,
        late_prompt=lax.axis_index(TOK) // POINTS == 1,
        first_core=lax.axis_index("c") == 0,
        visible=jnp.asarray(visible),
        masks=[jnp.asarray(np.arange(128)[None, :] == lane) for lane in range(6)],
        attn_unscaled=1.0 / attn_gain,
        mlp_unscaled=1.0 / mlp_gain,
        error_rows=lax.dynamic_slice_in_dim(sae_error, first_token, SEQ, 0).astype(F32),
        cot_rows=lax.dynamic_slice_in_dim(cotangent, first_token, SEQ, 0).astype(F32),
    )


def feat_part_rows(piece):
    return spread(piece, Z, NZ)


def feat_part_sums(partial):
    rows, width = partial.shape
    return added(swap(partial.astype(B16).reshape(NZ, rows // NZ, width), Z))


def local(
    layer_input,
    enc_weight,
    enc_bias,
    active,
    dec_weight,
    dec_bias,
    sae_error,
    positions,
    attn_gain,
    query_weight,
    kv_weight,
    out_weight,
    mlp_gain,
    gate_weight,
    up_weight,
    down_weight,
    cotangent,
):
    width = enc_weight.shape[1]
    hidden = gate_weight.shape[1]
    model_width = dec_weight.shape[1]

    out_rows = lax.all_gather(out_weight, "y", axis=0, tiled=True)
    first_sums = jnp.concatenate(
        [dot(layer_input, enc_weight).astype(B16), dot_t(cotangent, down_weight).astype(B16)],
        axis=1,
    ).reshape(NX * NC, SEQ, width + hidden)
    own_positions = jnp.broadcast_to(
        positions.reshape(1, SEQ, 1).astype(B16), (NX * NC, SEQ, 128)
    )
    blocks = swap(jnp.concatenate([first_sums, own_positions], axis=2), TOK)
    ready = prepared(attn_gain, mlp_gain, sae_error, cotangent)
    active_rows = active.reshape(POINTS, SEQ, width).astype(F32)
    turned_rows = jnp.concatenate(
        [turned(query_weight), placed_block(turned(kv_weight))], axis=0
    )
    blocks, ready, active_rows, gate_weight, up_weight, turned_rows = (
        lax.optimization_barrier(
            (blocks, ready, active_rows, gate_weight, up_weight, turned_rows)
        )
    )
    turned_rows = lax.all_gather(turned_rows, "y", axis=0, tiled=True)
    first_core, masks = ready["first_core"], ready["masks"]
    first_sums = added(blocks[:, :, : width + hidden])
    own_positions = lax.dynamic_index_in_dim(
        blocks[:, :, width + hidden], ready["own_prompt"], 0, keepdims=False
    ).astype(F32)
    frequency = (rope_base ** (-np.arange(HD // 2) * 2.0 / HD)).astype(np.float32)
    angles = own_positions[:, None] * frequency
    tables = [
        jnp.concatenate([table] * count, axis=0)
        for count in (NZ, NY)
        for table in (jnp.cos(angles), jnp.sin(angles))
    ]
    encoded = first_sums[:, :width]
    back_hidden = first_sums[:, width:]
    features = [
        active_rows[k] * ((k + 1) / POINTS * encoded + enc_bias) for k in range(POINTS)
    ]
    changes = [features[0]] + [features[k] - features[k - 1] for k in range(1, POINTS)]
    changes = jnp.concatenate(changes, axis=0)
    sent_rows = jnp.concatenate(
        features + [back_hidden.reshape(-1, width)], axis=0
    ).astype(B16)
    feature_rows = POINTS * SEQ
    own_rows = spread(sent_rows, "x", NX)
    gate_up_turned = jnp.concatenate([turned(gate_weight), turned(up_weight)], axis=0)
    own_rows, changes, gate_up_turned, tables = lax.optimization_barrier(
        (own_rows, changes, gate_up_turned, tables)
    )
    gathered = both_cores(own_rows, first_core, sent_rows).reshape((NX * NC,) + sent_rows.shape)
    features = gathered[:, :feature_rows].reshape(-1, width)
    back_hidden = gathered[:, feature_rows:].reshape(NY, -1, width)
    decoded = dot(features, dec_weight).astype(B16).reshape(NY, -1, model_width)
    blocks = swap(jnp.concatenate([decoded, back_hidden], axis=1), "y")
    blocks, out_rows, gate_up_turned = lax.optimization_barrier(
        (blocks, out_rows, gate_up_turned)
    )
    gate_up_turned = lax.all_gather(gate_up_turned, "y", axis=0, tiled=True)
    chunk_rows = decoded.shape[1]
    decoded = added(blocks[:, :chunk_rows]).astype(B16).reshape(NZ, SEQ, model_width)
    decoded = added(swap(decoded, Z))
    hidden_in = decoded + dec_bias + ready["error_rows"]

    gained = feat_part_rows((hidden_in * attn_gain).astype(B16))
    squares = jnp.sum(
        jnp.square(gained.astype(F32) * ready["attn_unscaled"]), axis=1, keepdims=True
    )
    projections = tok_sums(
        jnp.concatenate(
            [dot_t(gained, turned_rows).astype(B16), split_column(masks, squares)], axis=1
        )
    )
    head_part = query_weight.shape[1]
    qkv_width = turned_rows.shape[0]
    scale_rows = lax.rsqrt(joined_column(projections[:, qkv_width:]) / D + epsilon)
    own_qkv = (projections[:, :qkv_width] * scale_rows).reshape(SEQ, NY, qkv_width // NY)
    kv_part = own_qkv.shape[2] - head_part
    own_keyval = own_qkv[:, :, head_part:].astype(B16).reshape(SEQ, NY * kv_part)
    keyval = jnp.broadcast_to(own_keyval[None], (QUAD,) + own_keyval.shape)
    keyval, blocks = lax.optimization_barrier((keyval, blocks))
    keyval = swap(keyval, "quad")
    back_hidden = blocks[:, chunk_rows:].reshape(NY, 2, SEQ, hidden)
    back_hidden = jnp.where(ready["late_prompt"], back_hidden[:, 1], back_hidden[:, 0])
    back_hidden = back_hidden.transpose(1, 0, 2).astype(F32)
    keyval, back_hidden = lax.optimization_barrier((keyval, back_hidden))
    keyval = keyval.reshape(QUAD, SEQ, NY, kv_part)
    attended, saved = attend(
        own_qkv[:, :, :head_part].reshape(SEQ, -1),
        keyval.transpose(1, 2, 0, 3).reshape(SEQ, -1).astype(F32),
        tables,
        ready["visible"],
    )
    attended, saved = lax.optimization_barrier((attended.astype(B16), saved))
    projected = feat_part_sums(dot(tok_rows(attended), out_rows))
    middle = hidden_in + projected

    gained = feat_part_rows((middle * mlp_gain).astype(B16))
    gained = gained.reshape(NX, NC, SEQ, model_width)
    gained = jnp.where(first_core, gained, gained[:, ::-1])

    def gate_up_product(rows):
        squares = jnp.sum(
            jnp.square(rows.astype(F32) * ready["mlp_unscaled"]), axis=1, keepdims=True
        )
        return jnp.concatenate(
            [dot_t(rows, gate_up_turned).astype(B16), split_column(masks, squares)], axis=1
        ).astype(F32)

    gate_up = tok_sums_core_first(gained.reshape(-1, model_width), gate_up_product)
    scale_mlp = lax.rsqrt(joined_column(gate_up[:, NY * 2 * hidden :]) / D + epsilon)
    gate_up = gate_up[:, : NY * 2 * hidden].reshape(SEQ, NY, 2 * hidden)
    gate_raw = gate_up[:, :, :hidden]
    up_raw = gate_up[:, :, hidden:]
    gate_value = gate_raw * scale_mlp[:, :, None]
    up_value = up_raw * scale_mlp[:, :, None]
    sigmoid_gate = jax.nn.sigmoid(gate_value)
    grad_gate = back_hidden * up_value * sigmoid_gate * (1.0 + gate_value * (1.0 - sigmoid_gate))
    grad_up = back_hidden * gate_value * sigmoid_gate
    grad_gate, grad_up = grad_gate.astype(B16), grad_up.astype(B16)
    meeting = jnp.sum(
        grad_gate.astype(F32) * gate_raw + grad_up.astype(F32) * up_raw, axis=(1, 2)
    )[:, None]
    mlp_grads = jnp.concatenate([grad_gate, grad_up], axis=2).reshape(SEQ, -1)
    mlp_grads = jnp.concatenate([mlp_grads, split_column(masks, scale_mlp, meeting)], axis=1)
    mlp_grads = both_cores(spread(mlp_grads, "x", NX), first_core, mlp_grads)
    mlp_width = NY * 2 * hidden
    back_second = feat_part_sums(
        jnp.concatenate(
            [
                dot(mlp_grads[:, :mlp_width], gate_up_turned).astype(B16),
                mlp_grads[:, mlp_width:],
            ],
            axis=1,
        )
    )
    extras = back_second[:, model_width:]
    scale_second = joined_column(extras) / NZ
    total = joined_column(extras, 2)

    weighted_second = back_second[:, :model_width] * mlp_gain
    grad_middle = (
        ready["cot_rows"]
        + scale_second * weighted_second
        - middle * scale_second**3 * (total / D)
    )
    gathered = feat_part_rows(grad_middle.astype(B16))
    grad_attended = tok_sums(dot_t(gathered, out_rows))
    grad_query, grad_keyval = attend_back(grad_attended, saved)
    grad_keyval = grad_keyval.astype(B16).reshape(SEQ, NY, QUAD, kv_part)
    grad_keyval = added(swap(grad_keyval.transpose(2, 0, 1, 3).reshape(QUAD, SEQ, -1), "quad"))
    attn_grads = jnp.concatenate(
        [grad_query.reshape(SEQ, NY, head_part), grad_keyval.reshape(SEQ, NY, kv_part)], axis=2
    )
    attn_grads = attn_grads.reshape(SEQ, qkv_width).astype(B16)
    meeting = jnp.sum(
        attn_grads.astype(F32) * projections[:, :qkv_width], axis=1, keepdims=True
    )
    gathered = tok_rows(
        jnp.concatenate([attn_grads, split_column(masks, meeting, scale_rows)], axis=1)
    )
    back_first = feat_part_sums(
        jnp.concatenate(
            [
                dot(gathered[:, :qkv_width], turned_rows).astype(B16),
                gathered[:, qkv_width:],
            ],
            axis=1,
        )
    )
    extras = back_first[:, model_width:]
    total = joined_column(extras)
    scale_first = joined_column(extras, 2) / NZ
    weighted_first = back_first[:, :model_width] * attn_gain
    grad_hidden = (
        grad_middle
        + scale_first * weighted_first
        - hidden_in * scale_first**3 * (total / D)
    )
    gathered = feat_rows(grad_hidden.astype(B16), first_core)
    feature_grads = tok_sums_core_first(gathered, lambda rows: dot_t(rows, dec_weight))
    return jnp.sum((feature_grads * changes).reshape(POINTS, SEQ, width), axis=0)


def solution(mesh):
    fine = Mesh(mesh.devices.reshape(NY, NZ // QUAD, QUAD, NX, NC), FEAT + TOK)
    in_specs = (
        P(None, TOK),
        P(TOK, FEAT),
        P(FEAT),
        P(TOK, FEAT),
        P(FEAT, TOK),
        P(TOK),
        P(None, TOK),
        P(TOK, None),
        P(TOK),
        P(TOK, FEAT),
        P(TOK, FEAT),
        P(FEAT, TOK),
        P(TOK),
        P(TOK, FEAT),
        P(TOK, FEAT),
        P(FEAT, TOK),
        P(None, TOK),
    )
    return jax.shard_map(
        local, mesh=fine, in_specs=in_specs, out_specs=P(TOK, FEAT), check_vma=False
    )
```

```python
import jax
import jax.numpy as jnp
import numpy as np
from jax import lax
from jax.sharding import Mesh
from jax.sharding import PartitionSpec as P

D = 8192
HD = 128
POINTS = 4
SEQ = 16
NY, NZ, NX, NC = 4, 8, 4, 2
QUAD = 4
Z = ("half", "quad")
FEAT = ("y", "half", "quad")
TOK = ("x", "c")

epsilon = 1e-05
rope_base = 500000.0
F32 = jnp.float32
B16 = jnp.bfloat16


def dot(left_side, right_side):
    return jnp.dot(left_side, right_side, preferred_element_type=F32)


def dot_t(left_side, right_side):
    return lax.dot_general(
        left_side, right_side, (((1,), (1,)), ((), ())), preferred_element_type=F32
    )


def exact(left_side, right_side, left_dim, right_dim):
    return lax.dot_general(
        left_side,
        right_side,
        (((left_dim,), (right_dim,)), ((), ())),
        precision=lax.Precision.HIGHEST,
        preferred_element_type=F32,
    )


def swap(blocks, axes):
    return lax.all_to_all(blocks, axes, 0, 0, tiled=True)


def spread(piece, axes, count):
    blocks = jnp.broadcast_to(piece[None], (count,) + piece.shape)
    return swap(lax.optimization_barrier(blocks), axes).reshape((-1,) + piece.shape[1:])


def added(blocks):
    return jnp.sum(blocks.astype(F32), axis=0)


def feat_sums(partial):
    rows, width = partial.shape
    blocks = swap(partial.astype(B16).reshape(NY, rows // NY, width), "y")
    blocks = added(blocks).astype(B16).reshape(NZ, rows // (NY * NZ), width)
    return added(swap(blocks, Z))


def feat_rows(piece, first_core=None):
    piece = spread(piece, Z, NZ)
    if first_core is not None:
        halves = piece.reshape((2, -1) + piece.shape[1:])
        piece = jnp.where(first_core, halves, halves[::-1]).reshape(piece.shape)
    return spread(piece, "y", NY)


def tok_sums(partial):
    rows, width = partial.shape
    return added(swap(partial.astype(B16).reshape(NX * NC, rows // (NX * NC), width), TOK))


def other_core(values):
    return lax.ppermute(values, "c", [(0, 1), (1, 0)])


def tok_sums_core_first(rows, product):
    blocks = rows.reshape(NX, NC, -1, rows.shape[-1])
    height = blocks.shape[2]
    if height == SEQ:
        sums = product(rows).astype(B16).reshape(NX, NC, height, -1)
        own, other = sums[:, 0], sums[:, 1]
    else:
        other = product(blocks[:, 1].reshape(NX * height, -1)).astype(B16)
        own = product(blocks[:, 0].reshape(NX * height, -1))
    received = other_core(other).astype(F32).reshape(NX, height, -1)
    own = (own.astype(F32).reshape(NX, height, -1) + received).astype(B16)
    return added(swap(own, "x"))


def tok_rows(piece):
    return spread(piece, TOK, NX * NC)


def both_cores(own, first_core, piece):
    own = own.reshape((NX,) + piece.shape)
    other = other_core(own)
    first = jnp.where(first_core, own, other)
    second = jnp.where(first_core, other, own)
    return jnp.stack([first, second], axis=1).reshape((-1,) + piece.shape[1:])


def split_column(masks, *columns):
    block = jnp.zeros((columns[0].shape[0], 128), F32)
    for index, values in enumerate(columns):
        high = lax.reduce_precision(values, 8, 7)
        block = jnp.where(masks[2 * index], high, block)
        block = jnp.where(masks[2 * index + 1], values - high, block)
    return block.astype(B16)


def lane_sums(values):
    parts = [values[:, start : start + 128] for start in range(0, values.shape[1], 128)]
    return sum(parts[1:], parts[0])


def joined_column(block, first=0):
    return block[:, first : first + 1].astype(F32) + block[:, first + 1 : first + 2].astype(F32)


def rotate(vectors, cosine, sine):
    half = vectors.shape[-1] // 2
    first, second = vectors[:, :half], vectors[:, half:]
    return jnp.concatenate(
        [first * cosine - second * sine, second * cosine + first * sine], axis=-1
    )


def stacked_heads(values):
    heads = values.shape[1] // HD
    return jnp.concatenate([values[:, h * HD : (h + 1) * HD] for h in range(heads)], axis=0)


def side_by_side(values):
    heads = values.shape[0] // SEQ
    return jnp.concatenate([values[h * SEQ : (h + 1) * SEQ] for h in range(heads)], axis=1)


def attend(query_rows, keyval_rows, tables, visible):
    half = keyval_rows.shape[1] // 2
    queries = rotate(stacked_heads(query_rows), tables[0], tables[1])
    keys = rotate(stacked_heads(keyval_rows[:, :half]), tables[2], tables[3])
    values = stacked_heads(keyval_rows[:, half:])
    scores = exact(queries, keys, 1, 1) * HD ** (-0.5)
    scores = jnp.where(visible, scores, -1e30)
    weights = jnp.exp(scores - jnp.max(scores, axis=-1, keepdims=True))
    weights = weights / jnp.sum(weights, axis=-1, keepdims=True)
    saved = (queries, keys, values, weights, tables)
    return side_by_side(exact(weights, values, 1, 0)), saved


def attend_back(grad_attended, saved):
    queries, keys, values, weights, tables = saved
    grads = stacked_heads(grad_attended)
    grad_values = exact(weights, grads, 0, 0)
    grad_weights = exact(grads, values, 1, 1)
    mean_grad = jnp.sum(grad_weights * weights, axis=-1, keepdims=True)
    grad_scores = weights * (grad_weights - mean_grad) * HD ** (-0.5)
    grad_queries = rotate(exact(grad_scores, keys, 1, 0), tables[0], -tables[1])
    grad_keys = rotate(exact(grad_scores, queries, 0, 0), tables[2], -tables[3])
    return side_by_side(grad_queries), jnp.concatenate(
        [side_by_side(grad_keys), side_by_side(grad_values)], axis=1
    )


def turned(weight):
    return dot_t(jnp.eye(weight.shape[1], dtype=B16), weight).astype(B16)


def placed_block(block):
    moves = []
    for source in range(NY * NZ):
        row, place = divmod(source, NZ)
        half = (place // 2) % 2
        moves.append((source, NZ * row + QUAD * half + 2 * (place // QUAD) + place % 2))
    return lax.ppermute(block, FEAT, moves)


def prepared(attn_gain, mlp_gain, sae_error, cotangent):
    feat = lax.axis_index(FEAT)
    first_token = (feat // POINTS) * SEQ
    row = np.arange(NZ * SEQ)
    key = np.arange(NY * SEQ)
    visible = (row[:, None] // (2 * SEQ) == key // SEQ) & (row[:, None] % SEQ >= key % SEQ)
    return dict(
        own_prompt=2 * lax.axis_index("y") + lax.axis_index(TOK) // POINTS,
        late_prompt=lax.axis_index(TOK) // POINTS == 1,
        first_core=lax.axis_index("c") == 0,
        visible=jnp.asarray(visible),
        masks=[jnp.asarray(np.arange(128)[None, :] == lane) for lane in range(6)],
        attn_unscaled=1.0 / attn_gain,
        mlp_unscaled=1.0 / mlp_gain,
        error_rows=lax.dynamic_slice_in_dim(sae_error, first_token, SEQ, 0).astype(F32),
        cot_rows=lax.dynamic_slice_in_dim(cotangent, first_token, SEQ, 0).astype(F32),
    )


def feat_part_rows(piece):
    return spread(piece, Z, NZ)


def feat_part_sums(partial):
    rows, width = partial.shape
    return added(swap(partial.astype(B16).reshape(NZ, rows // NZ, width), Z))


def local(
    layer_input,
    enc_weight,
    enc_bias,
    active,
    dec_weight,
    dec_bias,
    sae_error,
    positions,
    attn_gain,
    query_weight,
    kv_weight,
    out_weight,
    mlp_gain,
    gate_weight,
    up_weight,
    down_weight,
    cotangent,
):
    width = enc_weight.shape[1]
    hidden = gate_weight.shape[1]
    model_width = dec_weight.shape[1]

    out_rows = lax.all_gather(out_weight, "y", axis=0, tiled=True)
    first_sums = jnp.concatenate(
        [dot(layer_input, enc_weight).astype(B16), dot_t(cotangent, down_weight).astype(B16)],
        axis=1,
    ).reshape(NX * NC, SEQ, width + hidden)
    own_positions = jnp.broadcast_to(
        positions.reshape(1, SEQ, 1).astype(B16), (NX * NC, SEQ, 128)
    )
    blocks = swap(jnp.concatenate([first_sums, own_positions], axis=2), TOK)
    ready = prepared(attn_gain, mlp_gain, sae_error, cotangent)
    active_rows = active.reshape(POINTS, SEQ, width).astype(F32)
    turned_rows = jnp.concatenate(
        [turned(query_weight), placed_block(turned(kv_weight))], axis=0
    )
    blocks, ready, active_rows, gate_weight, up_weight, turned_rows = (
        lax.optimization_barrier(
            (blocks, ready, active_rows, gate_weight, up_weight, turned_rows)
        )
    )
    turned_rows = lax.all_gather(turned_rows, "y", axis=0, tiled=True)
    first_core, masks = ready["first_core"], ready["masks"]
    first_sums = added(blocks[:, :, : width + hidden])
    own_positions = lax.dynamic_index_in_dim(
        blocks[:, :, width + hidden], ready["own_prompt"], 0, keepdims=False
    ).astype(F32)
    frequency = (rope_base ** (-np.arange(HD // 2) * 2.0 / HD)).astype(np.float32)
    encoded = first_sums[:, :width]
    back_hidden = first_sums[:, width:]
    features = [
        active_rows[k] * ((k + 1) / POINTS * encoded + enc_bias) for k in range(POINTS)
    ]
    changes = [features[0]] + [features[k] - features[k - 1] for k in range(1, POINTS)]
    changes = jnp.concatenate(changes, axis=0)
    sent_rows = jnp.concatenate(
        features + [back_hidden.reshape(-1, width)], axis=0
    ).astype(B16)
    feature_rows = POINTS * SEQ
    sent_blocks = jnp.broadcast_to(sent_rows[None], (NX,) + sent_rows.shape)
    sent_blocks, own_positions = lax.optimization_barrier((sent_blocks, own_positions))
    own_rows = swap(sent_blocks, "x")
    angles = own_positions[:, None] * frequency
    tables = [
        jnp.concatenate([table] * count, axis=0)
        for count in (NZ, NY)
        for table in (jnp.cos(angles), jnp.sin(angles))
    ]
    gate_up_turned = jnp.concatenate([turned(gate_weight), turned(up_weight)], axis=0)
    own_rows, changes, gate_up_turned, tables = lax.optimization_barrier(
        (own_rows, changes, gate_up_turned, tables)
    )
    gathered = both_cores(own_rows, first_core, sent_rows).reshape((NX * NC,) + sent_rows.shape)
    features = gathered[:, :feature_rows].reshape(-1, width)
    back_hidden = gathered[:, feature_rows:].reshape(NY, -1, width)
    decoded = dot(features, dec_weight).astype(B16).reshape(NY, -1, model_width)
    blocks = swap(jnp.concatenate([decoded, back_hidden], axis=1), "y")
    blocks, out_rows, gate_up_turned = lax.optimization_barrier(
        (blocks, out_rows, gate_up_turned)
    )
    gate_up_turned = lax.all_gather(gate_up_turned, "y", axis=0, tiled=True)
    chunk_rows = decoded.shape[1]
    decoded = added(blocks[:, :chunk_rows]).astype(B16).reshape(NZ, SEQ, model_width)
    decoded = added(swap(decoded, Z))
    hidden_in = decoded + dec_bias + ready["error_rows"]

    gained = feat_part_rows((hidden_in * attn_gain).astype(B16))
    squares = lane_sums(jnp.square(gained.astype(F32) * ready["attn_unscaled"]))
    projections = tok_sums(
        jnp.concatenate(
            [dot_t(gained, turned_rows).astype(B16), squares.astype(B16)], axis=1
        )
    )
    head_part = query_weight.shape[1]
    qkv_width = turned_rows.shape[0]
    scale_rows = lax.rsqrt(
        jnp.sum(projections[:, qkv_width:], axis=1, keepdims=True) / D + epsilon
    )
    own_qkv = (projections[:, :qkv_width] * scale_rows).reshape(SEQ, NY, qkv_width // NY)
    kv_part = own_qkv.shape[2] - head_part
    own_keyval = own_qkv[:, :, head_part:].astype(B16).reshape(SEQ, NY * kv_part)
    keyval = jnp.broadcast_to(own_keyval[None], (QUAD,) + own_keyval.shape)
    keyval, blocks = lax.optimization_barrier((keyval, blocks))
    keyval = swap(keyval, "quad")
    back_hidden = blocks[:, chunk_rows:].reshape(NY, 2, SEQ, hidden)
    back_hidden = jnp.where(ready["late_prompt"], back_hidden[:, 1], back_hidden[:, 0])
    back_hidden = back_hidden.transpose(1, 0, 2).astype(F32)
    keyval, back_hidden = lax.optimization_barrier((keyval, back_hidden))
    keyval = keyval.reshape(QUAD, SEQ, NY, kv_part)
    attended, saved = attend(
        own_qkv[:, :, :head_part].reshape(SEQ, -1),
        keyval.transpose(1, 2, 0, 3).reshape(SEQ, -1).astype(F32),
        tables,
        ready["visible"],
    )
    scale_block = split_column(masks, jnp.zeros_like(scale_rows), scale_rows)
    attended, saved, scale_block = lax.optimization_barrier(
        (attended.astype(B16), saved, scale_block)
    )
    projected = feat_part_sums(dot(tok_rows(attended), out_rows))
    middle = hidden_in + projected

    gained = feat_part_rows((middle * mlp_gain).astype(B16))
    gained = gained.reshape(NX, NC, SEQ, model_width)
    gained = jnp.where(first_core, gained, gained[:, ::-1])

    def gate_up_product(rows):
        squares = lane_sums(jnp.square(rows.astype(F32) * ready["mlp_unscaled"]))
        return jnp.concatenate(
            [dot_t(rows, gate_up_turned).astype(B16), squares.astype(B16)], axis=1
        ).astype(F32)

    gate_up = tok_sums_core_first(gained.reshape(-1, model_width), gate_up_product)
    scale_mlp = lax.rsqrt(
        jnp.sum(gate_up[:, NY * 2 * hidden :], axis=1, keepdims=True) / D + epsilon
    )
    gate_up = gate_up[:, : NY * 2 * hidden].reshape(SEQ, NY, 2 * hidden)
    gate_raw = gate_up[:, :, :hidden]
    up_raw = gate_up[:, :, hidden:]
    gate_value = gate_raw * scale_mlp[:, :, None]
    up_value = up_raw * scale_mlp[:, :, None]
    sigmoid_gate = jax.nn.sigmoid(gate_value)
    grad_gate = back_hidden * up_value * sigmoid_gate * (1.0 + gate_value * (1.0 - sigmoid_gate))
    grad_up = back_hidden * gate_value * sigmoid_gate
    grad_gate, grad_up = grad_gate.astype(B16), grad_up.astype(B16)
    meeting = jnp.sum(
        grad_gate.astype(F32) * gate_raw + grad_up.astype(F32) * up_raw, axis=(1, 2)
    )[:, None]
    mlp_grads = jnp.concatenate([grad_gate, grad_up], axis=2).reshape(SEQ, -1)
    mlp_grads = jnp.concatenate([mlp_grads, split_column(masks, scale_mlp, meeting)], axis=1)
    mlp_grads = both_cores(spread(mlp_grads, "x", NX), first_core, mlp_grads)
    mlp_width = NY * 2 * hidden
    back_second = feat_part_sums(
        jnp.concatenate(
            [
                dot(mlp_grads[:, :mlp_width], gate_up_turned).astype(B16),
                mlp_grads[:, mlp_width:],
            ],
            axis=1,
        )
    )
    extras = back_second[:, model_width:]
    scale_second = joined_column(extras) / NZ
    total = joined_column(extras, 2)

    weighted_second = back_second[:, :model_width] * mlp_gain
    grad_middle = (
        ready["cot_rows"]
        + scale_second * weighted_second
        - middle * scale_second**3 * (total / D)
    )
    gathered = feat_part_rows(grad_middle.astype(B16))
    grad_attended = tok_sums(dot_t(gathered, out_rows))
    grad_query, grad_keyval = attend_back(grad_attended, saved)
    grad_keyval = grad_keyval.astype(B16).reshape(SEQ, NY, QUAD, kv_part)
    grad_keyval = added(swap(grad_keyval.transpose(2, 0, 1, 3).reshape(QUAD, SEQ, -1), "quad"))
    attn_grads = jnp.concatenate(
        [grad_query.reshape(SEQ, NY, head_part), grad_keyval.reshape(SEQ, NY, kv_part)], axis=2
    )
    attn_grads = attn_grads.reshape(SEQ, qkv_width).astype(B16)
    meeting = jnp.sum(
        attn_grads.astype(F32) * projections[:, :qkv_width], axis=1, keepdims=True
    )
    gathered = tok_rows(
        jnp.concatenate([attn_grads, split_column(masks, meeting) + scale_block], axis=1)
    )
    back_first = feat_part_sums(
        jnp.concatenate(
            [
                dot(gathered[:, :qkv_width], turned_rows).astype(B16),
                gathered[:, qkv_width:],
            ],
            axis=1,
        )
    )
    extras = back_first[:, model_width:]
    total = joined_column(extras)
    scale_first = joined_column(extras, 2) / NZ
    weighted_first = back_first[:, :model_width] * attn_gain
    grad_hidden = (
        grad_middle
        + scale_first * weighted_first
        - hidden_in * scale_first**3 * (total / D)
    )
    gathered = feat_rows(grad_hidden.astype(B16), first_core)
    feature_grads = tok_sums_core_first(gathered, lambda rows: dot_t(rows, dec_weight))
    return jnp.sum((feature_grads * changes).reshape(POINTS, SEQ, width), axis=0)


def solution(mesh):
    fine = Mesh(mesh.devices.reshape(NY, NZ // QUAD, QUAD, NX, NC), FEAT + TOK)
    in_specs = (
        P(None, TOK),
        P(TOK, FEAT),
        P(FEAT),
        P(TOK, FEAT),
        P(FEAT, TOK),
        P(TOK),
        P(None, TOK),
        P(TOK, None),
        P(TOK),
        P(TOK, FEAT),
        P(TOK, FEAT),
        P(FEAT, TOK),
        P(TOK),
        P(TOK, FEAT),
        P(TOK, FEAT),
        P(FEAT, TOK),
        P(None, TOK),
    )
    return jax.shard_map(
        local, mesh=fine, in_specs=in_specs, out_specs=P(TOK, FEAT), check_vma=False
    )
```
